32 devices in a mesh: ctx: 4 (over y, x), exp: 4 (over z), tp: 2 (over core).
Axes of the slice: x: 2, y: 2, z: 4, core: 2. Of those that a mesh axis runs over, the one named last changes fastest.
Arguments:
- queries: bfloat16 [512, 36864], P('ctx', ('exp', 'tp')), may hold values from -90 to 90
- latent_keys: bfloat16 [512, 576], P('ctx'), may hold values from -6 to 6
- block_order: int32 [4], replicated, may hold values from 0 to 3, each once
- moe_input: bfloat16 [512, 3584], P(('ctx', 'exp')), may hold values from -6 to 6
- routes: int32 [512, 2], P(('ctx', 'exp')), may hold values from 0 to 3, all different within a row; in each aligned block of 32 rows (0 to 31, 32 to 63, ...) at most 32 rows name the same one
- gate_weights: float32 [512, 2], P(('ctx', 'exp')), may hold values from 0.2 to 1
- w_gate: bfloat16 [4, 3584, 1024], P('exp', 'ctx', 'tp'), may hold values from -0.09375 to 0.09375
- w_up: bfloat16 [4, 3584, 1024], P('exp', 'ctx', 'tp'), may hold values from -0.09375 to 0.09375
- w_down: bfloat16 [4, 1024, 3584], P('exp', 'ctx', 'tp'), may hold values from -0.1875 to 0.1875
Outputs:
- context: bfloat16 [512, 32768], P('ctx', ('exp', 'tp'))
- moe_out: bfloat16 [512, 3584], P(('ctx', 'exp'), 'tp')
The draws below stay inside these ranges and needn't reach their ends.
Inputs may be any that keep to these rules, and one draw needn't show every extreme that they name: `routes`: within the 32 rows of one device no expert is named by more than 32 rows, and some expert reaches 32. `block_order`: each block index appears once.
All inputs are finite; a program needn't handle non-finite values.
Results may differ from the reference program's by a relative error of at most 0.0065.
Values may be sent and summed in bfloat16 or wider, within the bound.
A program may use at most 64 MiB of HBM per device.

```python
import math
import jax
import jax.numpy as jnp
import numpy as np
from jax import lax

LATENT = 512
ROPE = 64
HEADS = 64
D = 3584
FFE = 1024
TOPK = 2
TQ = 128
TOK_DEV = 32
SEQ = 512
EXPERTS = 4
MTOK = 512
CAP = 32
N_CTX = 4


def keys_base(key):
    normal_part = jnp.clip(jax.random.normal(jax.random.fold_in(key, 101), (SEQ, LATENT + ROPE), jnp.float32), -6.0, 6.0)
    return normal_part


def draw_latent_keys(key, part):
    normal_part = keys_base(key)
    return normal_part.astype(jnp.bfloat16)


def draw_queries(key, part):
    key = jax.random.fold_in(key, 8)
    full_width = LATENT + ROPE
    result = jnp.clip(jax.random.normal(key, (SEQ, HEADS, full_width), jnp.float32), -6.0, 6.0)
    return result.reshape(SEQ, HEADS * full_width).astype(jnp.bfloat16)


def block_levels(key, extent, shards, least, top_value):
    gain = 1.0
    for axis_at, shards_of in shards:
        heights = jax.random.uniform(jax.random.fold_in(jax.random.fold_in(key, 6), axis_at), (shards_of,), jnp.float32, least / len(shards), top_value / len(shards))
        gain = gain * jnp.repeat(jnp.exp(heights), extent[axis_at] // shards_of).reshape((-1,) + (1,) * (len(extent) - 1 - axis_at))
    return gain


def routed_block(rng, own, number, rows, number_of, top, limit, lean):
    sequence = jax.random.permutation(rng, number_of)
    packed, usual = load_shares(number_of, rows * top, limit, lean, True), load_shares(number_of, rows * top, limit, lean, False)
    places = jnp.arange(number_of)

    def named(tallies, offset_by):
        used = int((tallies > 0).sum())
        fixed = max(1, used // 4)
        shifted = fixed + (places - fixed + offset_by * (used - fixed)) % max(1, number_of - fixed)
        return jnp.zeros((number_of,), jnp.int32).at[sequence[jnp.where(places < fixed, places, shifted)]].set(jnp.asarray(tallies, jnp.int32))

    tallies = jnp.where(number % 4 == 0, named(packed, number // 4), named(usual, number - number // 4 - 1))
    mixed = jax.random.permutation(jax.random.fold_in(own, 3), number_of)
    giver, receiver = mixed[0:number_of // 2 * 2:2], mixed[1:number_of // 2 * 2:2]
    room = jnp.minimum(tallies[giver] - 1, limit - tallies[receiver]) // 2
    room = jnp.where((giver == sequence[0]) | (receiver == sequence[0]) | (tallies[receiver] == 0), 0, jnp.maximum(room, 0))
    shifted = jax.random.randint(jax.random.fold_in(own, 4), (number_of // 2,), 0, 1 << 20) % (room + 1)
    tallies = tallies.at[giver].add(-shifted).at[receiver].add(shifted)
    members = jnp.searchsorted(jnp.cumsum(tallies), jnp.arange(rows * top), side="right").astype(jnp.int32)
    grid = members.reshape(top, rows).T
    grid = grid[jax.random.permutation(jax.random.fold_in(own, 1), rows)]
    offset_by = jax.random.randint(jax.random.fold_in(own, 2), (rows, 1), 0, top)
    return jnp.take_along_axis(grid, (jnp.arange(top)[None, :] + offset_by) % top, axis=1)


def load_shares(number_of, total, bound, slope, full):
    weights = [(1 << 20) // math.isqrt(standing ** slope) + 1 for standing in range(1, number_of + 1)]
    largest = bound if full else min(bound, max(-(-total // number_of), total * weights[0] // sum(weights)))
    least = 1 if total - largest >= number_of - 1 else 0
    counts, surplus = [largest] + [least] * (number_of - 1), total - largest - least * (number_of - 1)
    while surplus > 0:
        movable = [i for i in range(1, number_of) if counts[i] < largest] or [i for i in range(1, number_of) if counts[i] < bound]
        pool, remaining = sum([weights[i] for i in movable]), surplus
        for i in movable:
            addition = min(bound - counts[i], max(1, remaining * weights[i] // pool), surplus)
            counts[i] = counts[i] + addition
            surplus = surplus - addition
    return np.array(counts)


def bell_draw(rng, shape, width, limit, pieces=(), kind=jnp.bfloat16):
    drawn = width * jax.random.normal(rng, shape, jnp.float32)
    if pieces:
        drawn = drawn * block_levels(rng, shape, pieces, -0.22, 0.18)
    return jnp.clip(drawn, -limit, limit).astype(kind)


def setup_inputs(seed: int = 0) -> dict:
    keys = jax.random.split(jax.random.key(seed), 10)
    queries = draw_queries(jax.random.fold_in(keys[9], 71), 0)
    latent_keys = draw_latent_keys(jax.random.fold_in(keys[9], 71), 0)
    block_order = jax.random.permutation(keys[2], N_CTX).astype(jnp.int32)
    moe_input = bell_draw(keys[3], (MTOK, D), 1.0, 6.0, ((0, 16),))
    routes_keys = jax.random.split(jax.random.fold_in(keys[4], 1), MTOK // TOK_DEV)
    routes_turns = jax.random.permutation(jax.random.fold_in(keys[4], 3), MTOK // TOK_DEV)
    routes = jax.vmap(lambda own, number: routed_block(jax.random.fold_in(keys[4], 2), own, number, TOK_DEV, EXPERTS, TOPK, CAP, 2))(routes_keys, routes_turns).reshape((MTOK, TOPK))
    gate_weights = jnp.clip(0.2 + 0.8 * jax.random.uniform(keys[5], (MTOK, TOPK), jnp.float32) ** block_levels(keys[5], (MTOK, TOPK), ((0, 16),), -0.2, 0.2), 0.2, 1.0)
    w_gate = bell_draw(keys[6], (EXPERTS, D, FFE), D ** -0.5, 0.09375, ((0, 4), (1, 4), (2, 2)))
    w_up = bell_draw(keys[7], (EXPERTS, D, FFE), D ** -0.5, 0.09375, ((0, 4), (1, 4), (2, 2)))
    w_down = bell_draw(keys[8], (EXPERTS, FFE, D), FFE ** -0.5, 0.1875, ((0, 4), (1, 4), (2, 2)))
    return dict(queries=queries, latent_keys=latent_keys, block_order=block_order, moe_input=moe_input, routes=routes, gate_weights=gate_weights, w_gate=w_gate, w_up=w_up, w_down=w_down)


softmax_scale = 0.07216878364870323


def slot_table(route_rows, experts, capacity):
    flat_ids = route_rows.reshape(-1)
    one_hot = (flat_ids[:, None] == jnp.arange(experts, dtype=jnp.int32)[None, :]).astype(jnp.int32)
    earlier = jnp.cumsum(one_hot, axis=0) - one_hot
    ranking = jnp.sum(earlier * one_hot, axis=1)
    return (flat_ids * capacity + ranking).astype(jnp.int32)


def reference(queries, latent_keys, block_order, moe_input, routes, gate_weights, w_gate, w_up, w_down):
    full_width = LATENT + ROPE
    positions = (block_order[:, None] * TQ + jnp.arange(TQ, dtype=jnp.int32)[None, :]).reshape(SEQ)
    per_head = queries.reshape(SEQ, HEADS, full_width).transpose(1, 0, 2)
    values = latent_keys[:, :LATENT]
    visible = positions[None, :] <= positions[:, None]

    def one_head(head_queries):
        scores = jnp.dot(head_queries, latent_keys.T, preferred_element_type=jnp.float32) * softmax_scale
        masked = jnp.where(visible, scores, -jnp.inf)
        row_max = jnp.max(masked, axis=1, keepdims=True)
        weights = jnp.where(visible, jnp.exp(masked - row_max), 0.0)
        row_total = jnp.sum(weights, axis=1, keepdims=True)
        summed = jnp.dot(weights.astype(jnp.bfloat16), values, preferred_element_type=jnp.float32)
        return (summed / row_total).astype(jnp.bfloat16)

    heads_out = lax.map(one_head, per_head)
    context = heads_out.transpose(1, 0, 2).reshape(SEQ, HEADS * LATENT)

    gate_wide = w_gate.astype(jnp.float32)
    up_wide = w_up.astype(jnp.float32)
    down_wide = w_down.astype(jnp.float32)

    def one_block(block_index):
        first_row = block_index * TOK_DEV
        block_rows = lax.dynamic_slice_in_dim(moe_input, first_row, TOK_DEV, 0)
        block_routes = lax.dynamic_slice_in_dim(routes, first_row, TOK_DEV, 0)
        block_gates = lax.dynamic_slice_in_dim(gate_weights, first_row, TOK_DEV, 0)
        slot_index = slot_table(block_routes, EXPERTS, CAP)
        buffer = jnp.zeros((EXPERTS * CAP, D), jnp.bfloat16).at[slot_index].set(jnp.repeat(block_rows, TOPK, axis=0))
        grouped = buffer.reshape(EXPERTS, CAP, D).astype(jnp.float32)
        gate_proj = jnp.einsum("ecd,edf->ecf", grouped, gate_wide, precision=lax.Precision.HIGHEST)
        upward = jnp.einsum("ecd,edf->ecf", grouped, up_wide, precision=lax.Precision.HIGHEST)
        hidden = (jax.nn.silu(gate_proj) * upward).astype(jnp.bfloat16)
        expert_out = jnp.einsum("ecf,efd->ecd", hidden.astype(jnp.float32), down_wide, precision=lax.Precision.HIGHEST).astype(jnp.bfloat16)
        picked = expert_out.reshape(EXPERTS * CAP, D)[slot_index].astype(jnp.float32).reshape(TOK_DEV, TOPK, D)
        return jnp.sum(picked * block_gates[:, :, None], axis=1).astype(jnp.bfloat16)

    moe_out = lax.map(one_block, jnp.arange(MTOK // TOK_DEV, dtype=jnp.int32)).reshape(MTOK, D)
    return context, moe_out
```

```python
import functools

import jax
import jax.numpy as jnp
from jax import lax
from jax.experimental import pallas as pl
from jax.experimental.pallas import tpu as pltpu
from jax.sharding import PartitionSpec as P

LATENT = 512
ROPE = 64
LANES = 128
MESH = pl.DeviceIdType.MESH

softmax_scale = 0.07216878364870323
very_negative = -1e30


def kernel(
    n_ctx, n_exp,
    q_hbm, k_ref, order_ref, x_ref, routes_ref, gates_ref, wg_hbm, wu_hbm, wd_hbm,
    context_ref, moe_ref,
    q_ref, wg_ref, wu_ref, wd_ref,
    staged, rows, keys, gu_out, gu_in, hidden, dn_out, dn_in, z_out, z_in, home,
    load_sem,
    xs_s, xs_r, xz_s, xz_r, xc_s, xc_r, k_s, k_r, kc_s, kc_r,
    gu_s, gu_r, h_s, h_r, dn_s, dn_r, zz_s, zz_r,
):
    c, e, t = lax.axis_index("ctx"), lax.axis_index("exp"), lax.axis_index("tp")
    other = 1 - t
    width = wg_ref.shape[0]
    slice_width = wd_ref.shape[0]
    slices = wg_ref.shape[1] // slice_width
    tokens = x_ref.shape[0]
    half = tokens // 2
    block = k_ref.shape[0]
    chunk = n_ctx * tokens
    full_width = LATENT + ROPE
    heads = q_ref.shape[1] // full_width

    def ctx_at(step):
        return lax.rem(c + step, n_ctx)

    def exp_at(step):
        return lax.rem(e + step, n_exp)

    loads = [
        pltpu.make_async_copy(src, dst, load_sem.at[i])
        for i, (src, dst) in enumerate(
            ((wg_hbm, wg_ref), (wu_hbm, wu_ref), (q_hbm, q_ref), (wd_hbm, wd_ref))
        )
    ]
    for load in loads:
        load.start()

    barrier = pltpu.get_barrier_semaphore()
    for step in range(1, n_ctx):
        pl.semaphore_signal(barrier, inc=1, device_id={"ctx": ctx_at(step)}, device_id_type=MESH)
    for step in range(1, n_exp):
        pl.semaphore_signal(barrier, inc=1, device_id={"exp": exp_at(step)}, device_id_type=MESH)
    pl.semaphore_signal(barrier, inc=1, device_id={"tp": other}, device_id_type=MESH)

    lane = lax.broadcasted_iota(jnp.int32, (tokens, LANES), 1)
    expert_lane = lax.rem(lane, n_exp)
    dense = jnp.zeros((tokens, LANES), jnp.float32)
    for j in range(routes_ref.shape[1]):
        dense += jnp.where(routes_ref[:, j : j + 1] == expert_lane, gates_ref[:, j : j + 1], 0.0)
    high = dense.astype(jnp.bfloat16).astype(jnp.float32)
    packed = jnp.where(
        lane < n_exp, high, jnp.where(lane < 2 * n_exp, dense - high, 0.0)
    ).astype(jnp.bfloat16)
    for d in range(n_ctx):
        for part in range(2):
            span = slice(part * half, (part + 1) * half)
            staged[d, part, :, :width] = x_ref[span, d * width : (d + 1) * width]
            staged[d, part, :, width:] = packed[span, :]
    rows[e, c, t] = staged[c, t]
    keys[c, t] = k_ref[pl.ds(pl.multiple_of(t * (block // 2), block // 2), block // 2), :]

    pl.semaphore_wait(barrier, n_ctx + n_exp - 1)

    sends = []

    def send(src, dst, s_sem, r_sem, where):
        copy = pltpu.make_async_remote_copy(
            src_ref=src, dst_ref=dst, send_sem=s_sem, recv_sem=r_sem,
            device_id=where, device_id_type=MESH,
        )
        copy.start()
        return copy

    def arrived(dst, s_sem, r_sem, where):
        pltpu.make_async_remote_copy(
            src_ref=dst, dst_ref=dst, send_sem=s_sem, recv_sem=r_sem,
            device_id=where, device_id_type=MESH,
        ).wait_recv()

    core = {"tp": other}
    for step in range(1, n_ctx):
        d = ctx_at(step)
        sends.append(send(staged.at[d, t], rows.at[e, c, t], xs_s.at[step], xs_r.at[c], {"ctx": d}))
    for step in range(1, n_ctx):
        d = ctx_at(step)
        sends.append(send(keys.at[c, t], keys.at[c, t], k_s.at[step], k_r.at[c], {"ctx": d}))
    for step in range(1, n_ctx):
        d = ctx_at(step)
        arrived(rows.at[e, d, t], xs_s.at[step], xs_r.at[d], {"ctx": d})
    for step in range(1, n_exp):
        d = exp_at(step)
        sends.append(send(rows.at[e, :, t], rows.at[e, :, t], xz_s.at[step], xz_r.at[e], {"exp": d}))

    def share_chunk(i):
        source = exp_at(i)
        if i:
            arrived(rows.at[source, :, t], xz_s.at[i], xz_r.at[source], {"exp": source})
        sends.append(
            send(rows.at[source, :, t], rows.at[source, :, t], xc_s.at[i], xc_r.at[i], core)
        )

    def project(i):
        source = exp_at(i)
        arrived(rows.at[source, :, other], xc_s.at[i], xc_r.at[i], core)
        x = rows[source].reshape(chunk, width + LANES)[:, :width]
        for s in range(slices):
            columns = slice(s * slice_width, (s + 1) * slice_width)
            for at, weight in ((0, wg_ref), (slice_width, wu_ref)):
                gu_out[i, s, :, at : at + slice_width] = jnp.dot(
                    x, weight[:, columns], preferred_element_type=jnp.float32
                ).astype(jnp.bfloat16)
            d = slices * t + s

            @pl.when(d != c)
            def _():
                send(gu_out.at[i, s], gu_in.at[i, c], gu_s.at[i, s], gu_r.at[i, c], {"ctx": d})

    def down(i):
        source = exp_at(i)

        @pl.when(t == c // slices)
        def _():
            total = gu_out[i, lax.rem(c, slices)].astype(jnp.float32)
            for step in range(1, n_ctx):
                d = ctx_at(step)
                arrived(gu_in.at[i, d], gu_s.at[i, 0], gu_r.at[i, d], {"ctx": d})
                total += gu_in[i, d].astype(jnp.float32)
            gate, up = total[:, :slice_width], total[:, slice_width:]
            hidden[i] = (gate * jax.nn.sigmoid(gate) * up).astype(jnp.bfloat16)
            send(hidden.at[i], hidden.at[i], h_s.at[i], h_r.at[i], core)

        @pl.when(t != c // slices)
        def _():
            arrived(hidden.at[i], h_s.at[i], h_r.at[i], core)

        gate_lane = lax.broadcasted_iota(jnp.int32, (chunk, LANES), 1)
        table = rows[source].reshape(chunk, width + LANES)[:, width:].astype(jnp.float32)
        mine = (gate_lane == e) | (gate_lane == n_exp + e)
        scale = jnp.sum(jnp.where(mine, table, 0.0), axis=1, keepdims=True)
        units = hidden[i]
        out_width = wd_ref.shape[1]
        tile = 256 if out_width % 256 == 0 else LANES
        for at in range(0, out_width, tile):
            produced = jnp.dot(units, wd_ref[:, at : at + tile], preferred_element_type=jnp.float32)
            dn_out[i, :, :, at : at + tile] = (
                (produced * scale).astype(jnp.bfloat16).reshape(n_ctx, tokens, tile)
            )
        for step in range(1, n_ctx):
            d = ctx_at(step)
            sends.append(
                send(dn_out.at[i, d], dn_in.at[i, c], dn_s.at[i, step], dn_r.at[i, c], {"ctx": d})
            )

    def combine(i):
        for step in range(1, n_ctx):
            d = ctx_at(step)
            arrived(dn_in.at[i, d], dn_s.at[i, step], dn_r.at[i, d], {"ctx": d})
        total = dn_out[i, c].astype(jnp.float32)
        for step in range(1, n_ctx):
            total += dn_in[i, ctx_at(step)].astype(jnp.float32)
        if i == 0:
            home[...] = total
        else:
            z_out[i] = total.astype(jnp.bfloat16)
            sends.append(
                send(z_out.at[i], z_in.at[e], zz_s.at[i], zz_r.at[e], {"exp": exp_at(i)})
            )

    def gather_keys():
        for step in range(1, n_ctx):
            d = ctx_at(step)
            arrived(keys.at[d, t], k_s.at[step], k_r.at[d], {"ctx": d})
        sends.append(send(keys.at[:, t], keys.at[:, t], kc_s, kc_r, core))

    def mask():
        own = order_ref[c] * block + lax.broadcasted_iota(jnp.int32, (block, block), 0)
        at = lax.broadcasted_iota(jnp.int32, (block, block), 1)
        return jnp.concatenate(
            [order_ref[d] * block + at <= own for d in range(n_ctx)], axis=1
        )

    def attend(first, last):
        visible = mask()
        key_rows = keys[...].reshape(n_ctx * block, full_width)
        for h in range(first, last):
            scores = lax.dot_general(
                q_ref[:, h * full_width : (h + 1) * full_width], key_rows,
                (((1,), (1,)), ((), ())), preferred_element_type=jnp.float32,
            ) * softmax_scale
            masked = jnp.where(visible, scores, very_negative)
            top = jnp.max(masked, axis=1, keepdims=True)
            weights = jnp.where(visible, jnp.exp(masked - top), 0.0)
            total = jnp.sum(weights, axis=1, keepdims=True)
            summed = jnp.dot(
                weights.astype(jnp.bfloat16), key_rows[:, :LATENT],
                preferred_element_type=jnp.float32,
            )
            context_ref[:, h * LATENT : (h + 1) * LATENT] = (summed / total).astype(jnp.bfloat16)

    share_chunk(0)
    gather_keys()
    loads[0].wait()
    loads[1].wait()
    project(0)
    loads[2].wait()
    arrived(keys.at[:, other], kc_s, kc_r, core)
    cut = [heads * k // 4 for k in range(5)]
    attend(cut[0], cut[2])
    loads[3].wait()
    for i in range(1, n_exp + 2):
        if i < n_exp:
            share_chunk(i)
            if i == 1:
                attend(cut[2], cut[3])
            if i == 2:
                attend(cut[3], cut[4])
            project(i)
        if 0 <= i - 1 < n_exp:
            down(i - 1)
        if 0 <= i - 2 < n_exp:
            combine(i - 2)

    result = home[...]
    for step in range(1, n_exp):
        d = exp_at(step)
        arrived(z_in.at[d], zz_s.at[step], zz_r.at[d], {"exp": d})
        result += z_in[d].astype(jnp.float32)
    moe_ref[...] = result.astype(moe_ref.dtype)

    for copy in sends:
        copy.wait_send()
    for i in range(n_exp):
        for s in range(slices):
            d = slices * t + s

            @pl.when(d != c)
            def _():
                pltpu.make_async_remote_copy(
                    src_ref=gu_out.at[i, s], dst_ref=gu_in.at[i, c], send_sem=gu_s.at[i, s],
                    recv_sem=gu_r.at[i, c], device_id={"ctx": d}, device_id_type=MESH,
                ).wait_send()

        @pl.when(t == c // slices)
        def _():
            pltpu.make_async_remote_copy(
                src_ref=hidden.at[i], dst_ref=hidden.at[i], send_sem=h_s.at[i],
                recv_sem=h_r.at[i], device_id=core, device_id_type=MESH,
            ).wait_send()


def fused_body(n_ctx, n_exp, *args):
    queries, latent_keys, block_order, moe_input, routes, gate_weights, w_gate, w_up, w_down = args
    wg, wu, wd = w_gate[0], w_up[0], w_down[0]
    block, q_width = queries.shape
    heads = q_width // (LATENT + ROPE)
    tokens = moe_input.shape[0]
    width, units = wg.shape
    slice_width, out_width = wd.shape
    slices = units // slice_width
    chunk = n_ctx * tokens
    bf16, f32 = jnp.bfloat16, jnp.float32
    vmem = pl.BlockSpec(memory_space=pltpu.VMEM)
    smem = pl.BlockSpec(memory_space=pltpu.SMEM)
    anywhere = pl.BlockSpec(memory_space=pl.ANY)
    dma = pltpu.SemaphoreType.DMA
    by_ctx, by_exp = dma((n_ctx,)), dma((n_exp,))
    both = dma((n_exp, n_ctx))
    return pl.pallas_call(
        functools.partial(kernel, n_ctx, n_exp),
        out_shape=(
            jax.ShapeDtypeStruct((block, heads * LATENT), bf16),
            jax.ShapeDtypeStruct((tokens, out_width), bf16),
        ),
        in_specs=[anywhere, vmem, smem, vmem, vmem, vmem, anywhere, anywhere, anywhere],
        out_specs=(vmem, vmem),
        scratch_shapes=[
            pltpu.VMEM(queries.shape, bf16),
            pltpu.VMEM(wg.shape, bf16),
            pltpu.VMEM(wu.shape, bf16),
            pltpu.VMEM(wd.shape, bf16),
            pltpu.VMEM((n_ctx, 2, tokens // 2, width + LANES), bf16),
            pltpu.VMEM((n_exp, n_ctx, 2, tokens // 2, width + LANES), bf16),
            pltpu.VMEM((n_ctx, 2, block // 2, LATENT + ROPE), bf16),
            pltpu.VMEM((n_exp, slices, chunk, 2 * slice_width), bf16),
            pltpu.VMEM((n_exp, n_ctx, chunk, 2 * slice_width), bf16),
            pltpu.VMEM((n_exp, chunk, slice_width), bf16),
            pltpu.VMEM((n_exp, n_ctx, tokens, out_width), bf16),
            pltpu.VMEM((n_exp, n_ctx, tokens, out_width), bf16),
            pltpu.VMEM((n_exp, tokens, out_width), bf16),
            pltpu.VMEM((n_exp, tokens, out_width), bf16),
            pltpu.VMEM((tokens, out_width), f32),
            dma((4,)),
            by_ctx, by_ctx, by_exp, by_exp, by_exp, by_exp, by_ctx, by_ctx, dma, dma,
            dma((n_exp, slices)), both, by_exp, by_exp, both, both, by_exp, by_exp,
        ],
        compiler_params=pltpu.CompilerParams(
            collective_id=0, has_side_effects=True, vmem_limit_bytes=48 * 1024 * 1024
        ),
    )(queries, latent_keys, block_order, moe_input, routes, gate_weights, wg, wu, wd)


def passed_along(block, axis, distance):
    devices = range(lax.axis_size(axis))
    route = [((i - distance) % len(devices), i) for i in devices]
    return lax.ppermute(block, axis, route)


def slot_table(route_rows, experts, capacity):
    flat_ids = route_rows.reshape(-1)
    one_hot = (flat_ids[:, None] == jnp.arange(experts, dtype=jnp.int32)[None, :]).astype(jnp.int32)
    earlier = jnp.cumsum(one_hot, axis=0) - one_hot
    ranking = jnp.sum(earlier * one_hot, axis=1)
    return flat_ids * capacity + ranking


def body(queries, latent_keys, block_order, moe_input, routes, gate_weights, w_gate, w_up, w_down):
    full_gate, full_up, full_down = (
        lax.all_gather(w_gate, "ctx", axis=1, tiled=True),
        lax.all_gather(w_up, "ctx", axis=1, tiled=True),
        lax.all_gather(w_down, "ctx", axis=1, tiled=True),
    )
    full_width = LATENT + ROPE
    block_len = queries.shape[0]
    heads_here = queries.shape[1] // full_width
    per_head = queries.reshape(block_len, heads_here, full_width)
    cycle_size = lax.axis_size("ctx")
    position = lax.axis_index("ctx")
    offsets = jnp.arange(block_len, dtype=jnp.int32)
    own_block = block_order[position]
    own_pos = own_block * block_len + offsets

    def attend(running, key_block, source):
        source_block = block_order[source]
        top_old, total_old, summed_old = running
        key_pos = source_block * block_len + offsets
        visible = (key_pos[None, :] <= own_pos[:, None]) & True
        scores = (
            jnp.einsum("thc,uc->thu", per_head, key_block, preferred_element_type=jnp.float32)
            * softmax_scale
        )
        masked = jnp.where(visible[:, None, :], scores, very_negative)
        top_new = jnp.maximum(top_old, jnp.max(masked, axis=-1))
        weights = jnp.where(visible[:, None, :], jnp.exp(masked - top_new[:, :, None]), 0.0)
        factor = jnp.exp(top_old - top_new)
        total_new = total_old * factor + jnp.sum(weights, axis=-1)
        summed_new = summed_old * factor[:, :, None] + jnp.einsum(
            "thu,uc->thc",
            weights.astype(jnp.bfloat16),
            key_block[:, :LATENT],
            preferred_element_type=jnp.float32,
        )
        return (top_new, total_new, summed_new)

    initial = (
        jnp.full((block_len, heads_here), very_negative, jnp.float32),
        jnp.zeros((block_len, heads_here), jnp.float32),
        jnp.zeros((block_len, heads_here, LATENT), jnp.float32),
    )
    running = attend(initial, latent_keys, position)

    def step_forward(step_index, carried):
        state_now, ahead_keys = carried
        ahead_keys = passed_along(ahead_keys, "ctx", 1)
        state_now = attend(state_now, ahead_keys, (position - step_index) % cycle_size)
        return (state_now, ahead_keys)

    finished = lax.fori_loop(1, cycle_size, step_forward, (running, latent_keys))
    top_score, row_total, summed = finished[0]
    context = (
        (summed / row_total[:, :, None])
        .astype(jnp.bfloat16)
        .reshape(block_len, heads_here * LATENT)
    )
    tokens_here = moe_input.shape[0]
    top_count = routes.shape[1]
    owners = lax.axis_size("exp")
    experts = w_gate.shape[0] * owners
    capacity = min(tokens_here, 2 * tokens_here * top_count // experts)
    model_width = moe_input.shape[1]
    half_width = w_down.shape[2]
    slot_index = slot_table(routes, experts, capacity)
    outgoing = (
        jnp.zeros((experts * capacity, model_width), jnp.bfloat16)
        .at[slot_index]
        .set(jnp.repeat(moe_input, top_count, axis=0))
    )
    outgoing = outgoing.reshape(owners, capacity, model_width)
    arrived = lax.all_to_all(outgoing, "exp", split_axis=0, concat_axis=0, tiled=True)
    flat_rows = arrived.reshape(-1, model_width)
    gate_proj = jnp.dot(flat_rows, full_gate[0], preferred_element_type=jnp.float32)
    upward = jnp.dot(flat_rows, full_up[0], preferred_element_type=jnp.float32)
    hidden = (jax.nn.silu(gate_proj) * upward).astype(jnp.bfloat16)
    hidden_all = lax.all_gather(hidden, "tp", axis=1, tiled=True)
    produced_rows = jnp.dot(hidden_all, full_down[0], preferred_element_type=jnp.float32).astype(
        jnp.bfloat16
    )
    produced = produced_rows.reshape(arrived.shape[0], arrived.shape[1], half_width)
    returned = lax.all_to_all(produced, "exp", split_axis=0, concat_axis=0, tiled=True)
    picked = (
        returned.reshape(-1, half_width)[slot_index]
        .astype(jnp.float32)
        .reshape(tokens_here, top_count, half_width)
    )
    moe_out = jnp.sum(picked * gate_weights[:, :, None], axis=1).astype(jnp.bfloat16)
    return (context, moe_out)


def solution(mesh):
    in_specs = (
        P("ctx", ("exp", "tp")),
        P("ctx", None),
        P(),
        P(("ctx", "exp"), None),
        P(("ctx", "exp"), None),
        P(("ctx", "exp"), None),
        P("exp", "ctx", "tp"),
        P("exp", "ctx", "tp"),
        P("exp", "ctx", "tp"),
    )
    out_specs = (P("ctx", ("exp", "tp")), P(("ctx", "exp"), "tp"))
    n_ctx, n_exp, n_tp = mesh.shape["ctx"], mesh.shape["exp"], mesh.shape["tp"]

    def whole(*args):
        units_slice = args[8].shape[1] // n_ctx
        width = args[6].shape[1] // n_ctx
        fits = units_slice % LANES == 0 and width % LANES == 0 and n_ctx * n_exp <= 16 and n_tp == 2
        inner = functools.partial(fused_body, n_ctx, n_exp) if fits else body
        return split(inner)(*args)

    def split(inner):
        return jax.shard_map(
            inner, mesh=mesh, in_specs=in_specs, out_specs=out_specs, check_vma=False
        )

    return whole
```

```python
import functools

import jax
import jax.numpy as jnp
from jax import lax
from jax.experimental import pallas as pl
from jax.experimental.pallas import tpu as pltpu
from jax.sharding import PartitionSpec as P

LATENT = 512
ROPE = 64
LANES = 128
MESH = pl.DeviceIdType.MESH

softmax_scale = 0.07216878364870323
very_negative = -1e30


def kernel(
    n_ctx, n_exp,
    q_hbm, k_hbm, order_hbm, x_hbm, routes_hbm, gates_hbm, wg_hbm, wu_hbm, wd_hbm,
    context_ref, moe_ref,
    q_ref, k_ref, order_ref, x_ref, routes_ref, gates_ref, wg_ref, wu_ref, wd_ref,
    key_columns, values,
    staged, rows, keys, gu_out, gu_in, hidden, dn_out, dn_in, z_out, z_in, home,
    load_sem,
    xs_s, xs_r, xz_s, xz_r, xc_s, xc_r, k_s, k_r, kc_s, kc_r,
    gu_s, gu_r, h_s, h_r, dn_s, dn_r, zz_s, zz_r,
):
    c, e, t = lax.axis_index("ctx"), lax.axis_index("exp"), lax.axis_index("tp")
    other = 1 - t
    width = wg_ref.shape[0]
    slice_width = wd_ref.shape[0]
    slices = wg_ref.shape[1] // slice_width
    tokens = x_ref.shape[0]
    half = tokens // 2
    block = k_ref.shape[1]
    chunk = n_ctx * tokens
    full_width = LATENT + ROPE
    heads = q_ref.shape[1] // full_width

    def ctx_at(step):
        return lax.rem(c + step, n_ctx)

    def exp_at(step):
        return lax.rem(e + step, n_exp)

    loads = [
        pltpu.make_async_copy(src, dst, load_sem.at[i])
        for i, (src, dst) in enumerate(
            (
                (x_hbm, x_ref), (routes_hbm, routes_ref), (gates_hbm, gates_ref),
                (k_hbm, k_ref), (order_hbm, order_ref), (wg_hbm, wg_ref), (wu_hbm, wu_ref),
                (q_hbm, q_ref), (wd_hbm, wd_ref),
            )
        )
    ]
    for load in loads:
        load.start()

    barrier = pltpu.get_barrier_semaphore()
    for step in range(1, n_ctx):
        pl.semaphore_signal(barrier, inc=1, device_id={"ctx": ctx_at(step)}, device_id_type=MESH)
    for step in range(1, n_exp):
        pl.semaphore_signal(barrier, inc=1, device_id={"exp": exp_at(step)}, device_id_type=MESH)
    pl.semaphore_signal(barrier, inc=1, device_id={"tp": other}, device_id_type=MESH)

    lane = lax.broadcasted_iota(jnp.int32, (tokens, LANES), 1)
    expert_lane = lax.rem(lane, n_exp)
    square = (tokens, tokens)
    on_diagonal = lax.broadcasted_iota(jnp.int32, square, 0) == lax.broadcasted_iota(
        jnp.int32, square, 1
    )
    for load in loads[:4]:
        load.wait()
    dense = jnp.zeros((tokens, LANES), jnp.float32)
    for expert in range(n_exp):
        line = jnp.sum(
            jnp.where(routes_ref[...] == expert, gates_ref[...], 0.0), axis=0, keepdims=True
        )
        column = jnp.sum(
            jnp.where(on_diagonal, jnp.broadcast_to(line, square), 0.0), axis=1, keepdims=True
        )
        dense += jnp.where(expert_lane == expert, column, 0.0)
    high = dense.astype(jnp.bfloat16).astype(jnp.float32)
    packed = jnp.where(
        lane < n_exp, high, jnp.where(lane < 2 * n_exp, dense - high, 0.0)
    ).astype(jnp.bfloat16)
    for d in range(n_ctx):
        for part in range(2):
            span = slice(part * half, (part + 1) * half)
            staged[d, part, :, :width] = x_ref[span, d * width : (d + 1) * width]
            staged[d, part, :, width:] = packed[span, :]
    rows[e, c, t] = staged[c, t]
    part_width = full_width // 2
    keys[c, t] = k_ref[pl.ds(pl.multiple_of(t * part_width, part_width), part_width), :]

    pl.semaphore_wait(barrier, n_ctx + n_exp - 1)

    sends = []

    def send(src, dst, s_sem, r_sem, where):
        copy = pltpu.make_async_remote_copy(
            src_ref=src, dst_ref=dst, send_sem=s_sem, recv_sem=r_sem,
            device_id=where, device_id_type=MESH,
        )
        copy.start()
        return copy

    def arrived(dst, s_sem, r_sem, where):
        pltpu.make_async_remote_copy(
            src_ref=dst, dst_ref=dst, send_sem=s_sem, recv_sem=r_sem,
            device_id=where, device_id_type=MESH,
        ).wait_recv()

    core = {"tp": other}
    for step in range(1, n_ctx):
        d = ctx_at(step)
        sends.append(send(staged.at[d, t], rows.at[e, c, t], xs_s.at[step], xs_r.at[c], {"ctx": d}))
    for step in range(1, n_ctx):
        d = ctx_at(step)
        sends.append(send(keys.at[c, t], keys.at[c, t], k_s.at[step], k_r.at[c], {"ctx": d}))
    for step in range(1, n_ctx):
        d = ctx_at(step)
        arrived(rows.at[e, d, t], xs_s.at[step], xs_r.at[d], {"ctx": d})
    for step in range(1, n_exp):
        d = exp_at(step)
        sends.append(send(rows.at[e, :, t], rows.at[e, :, t], xz_s.at[step], xz_r.at[e], {"exp": d}))

    def share_chunk(i):
        source = exp_at(i)
        if i:
            arrived(rows.at[source, :, t], xz_s.at[i], xz_r.at[source], {"exp": source})
        sends.append(
            send(rows.at[source, :, t], rows.at[source, :, t], xc_s.at[i], xc_r.at[i], core)
        )

    def project(i):
        source = exp_at(i)
        arrived(rows.at[source, :, other], xc_s.at[i], xc_r.at[i], core)
        x = rows[source].reshape(chunk, width + LANES)[:, :width]
        for s in range(slices):
            columns = slice(s * slice_width, (s + 1) * slice_width)
            for at, weight in ((0, wg_ref), (slice_width, wu_ref)):
                gu_out[i, s, :, at : at + slice_width] = jnp.dot(
                    x, weight[:, columns], preferred_element_type=jnp.float32
                ).astype(jnp.bfloat16)
            d = slices * t + s

            @pl.when(d != c)
            def _():
                send(gu_out.at[i, s], gu_in.at[i, c], gu_s.at[i, s], gu_r.at[i, c], {"ctx": d})

    def down(i):
        source = exp_at(i)

        @pl.when(t == c // slices)
        def _():
            total = gu_out[i, lax.rem(c, slices)].astype(jnp.float32)
            for step in range(1, n_ctx):
                d = ctx_at(step)
                arrived(gu_in.at[i, d], gu_s.at[i, 0], gu_r.at[i, d], {"ctx": d})
                total += gu_in[i, d].astype(jnp.float32)
            gate, up = total[:, :slice_width], total[:, slice_width:]
            hidden[i] = (gate * jax.nn.sigmoid(gate) * up).astype(jnp.bfloat16)
            send(hidden.at[i], hidden.at[i], h_s.at[i], h_r.at[i], core)

        @pl.when(t != c // slices)
        def _():
            arrived(hidden.at[i], h_s.at[i], h_r.at[i], core)

        gate_lane = lax.broadcasted_iota(jnp.int32, (chunk, LANES), 1)
        table = rows[source].reshape(chunk, width + LANES)[:, width:].astype(jnp.float32)
        mine = (gate_lane == e) | (gate_lane == n_exp + e)
        scale = jnp.sum(jnp.where(mine, table, 0.0), axis=1, keepdims=True)
        units = hidden[i]
        out_width = wd_ref.shape[1]
        tile = 256 if out_width % 256 == 0 else LANES
        for at in range(0, out_width, tile):
            produced = jnp.dot(units, wd_ref[:, at : at + tile], preferred_element_type=jnp.float32)
            dn_out[i, :, :, at : at + tile] = (
                (produced * scale).astype(jnp.bfloat16).reshape(n_ctx, tokens, tile)
            )
        for step in range(1, n_ctx):
            d = ctx_at(step)
            sends.append(
                send(dn_out.at[i, d], dn_in.at[i, c], dn_s.at[i, step], dn_r.at[i, c], {"ctx": d})
            )

    def combine(i):
        for step in range(1, n_ctx):
            d = ctx_at(step)
            arrived(dn_in.at[i, d], dn_s.at[i, step], dn_r.at[i, d], {"ctx": d})
        total = dn_out[i, c].astype(jnp.float32)
        for step in range(1, n_ctx):
            total += dn_in[i, ctx_at(step)].astype(jnp.float32)
        if i == 0:
            home[...] = total
        else:
            z_out[i] = total.astype(jnp.bfloat16)
            sends.append(
                send(z_out.at[i], z_in.at[e], zz_s.at[i], zz_r.at[e], {"exp": exp_at(i)})
            )

    def gather_keys():
        for step in range(1, n_ctx):
            d = ctx_at(step)
            arrived(keys.at[d, t], k_s.at[step], k_r.at[d], {"ctx": d})
        sends.append(send(keys.at[:, t], keys.at[:, t], kc_s, kc_r, core))

    def mask():
        own = order_ref[c] * block + lax.broadcasted_iota(jnp.int32, (block, block), 0)
        at = lax.broadcasted_iota(jnp.int32, (block, block), 1)
        return jnp.concatenate(
            [order_ref[d] * block + at <= own for d in range(n_ctx)], axis=1
        )

    def attend(first, last):
        visible = mask()
        for h in range(first, last):
            scores = jnp.dot(
                q_ref[:, h * full_width : (h + 1) * full_width], key_columns[...],
                preferred_element_type=jnp.float32,
            ) * softmax_scale
            masked = jnp.where(visible, scores, very_negative)
            top = jnp.max(masked, axis=1, keepdims=True)
            weights = jnp.where(visible, jnp.exp(masked - top), 0.0)
            total = jnp.sum(weights, axis=1, keepdims=True)
            summed = jnp.dot(
                weights.astype(jnp.bfloat16), values[...], preferred_element_type=jnp.float32
            )
            context_ref[:, h * LATENT : (h + 1) * LATENT] = (summed / total).astype(jnp.bfloat16)

    share_chunk(0)
    gather_keys()
    loads[5].wait()
    loads[6].wait()
    project(0)
    loads[4].wait()
    loads[7].wait()
    arrived(keys.at[:, other], kc_s, kc_r, core)
    for d in range(n_ctx):
        block_keys = keys[d].reshape(full_width, block)
        key_columns[:, d * block : (d + 1) * block] = block_keys
        values[d * block : (d + 1) * block, :] = block_keys[:LATENT, :].T
    cut = [heads * k // 4 for k in range(5)]
    attend(cut[0], cut[2])
    loads[8].wait()
    down(0)
    for i in range(1, n_exp):
        share_chunk(i)
        if i <= 2:
            attend(cut[i + 1], cut[i + 2])
        project(i)
    for i in range(1, n_exp):
        down(i)
        combine(i - 1)
    combine(n_exp - 1)

    result = home[...]
    for step in range(1, n_exp):
        d = exp_at(step)
        arrived(z_in.at[d], zz_s.at[step], zz_r.at[d], {"exp": d})
        result += z_in[d].astype(jnp.float32)
    moe_ref[...] = result.astype(moe_ref.dtype)

    for copy in sends:
        copy.wait_send()
    for i in range(n_exp):
        for s in range(slices):
            d = slices * t + s

            @pl.when(d != c)
            def _():
                pltpu.make_async_remote_copy(
                    src_ref=gu_out.at[i, s], dst_ref=gu_in.at[i, c], send_sem=gu_s.at[i, s],
                    recv_sem=gu_r.at[i, c], device_id={"ctx": d}, device_id_type=MESH,
                ).wait_send()

        @pl.when(t == c // slices)
        def _():
            pltpu.make_async_remote_copy(
                src_ref=hidden.at[i], dst_ref=hidden.at[i], send_sem=h_s.at[i],
                recv_sem=h_r.at[i], device_id=core, device_id_type=MESH,
            ).wait_send()


def fused_body(n_ctx, n_exp, *args):
    queries, latent_keys, block_order, moe_input, routes, gate_weights, w_gate, w_up, w_down = args
    wg, wu, wd = w_gate[0], w_up[0], w_down[0]
    block, q_width = queries.shape
    heads = q_width // (LATENT + ROPE)
    tokens = moe_input.shape[0]
    width, units = wg.shape
    slice_width, out_width = wd.shape
    slices = units // slice_width
    chunk = n_ctx * tokens
    bf16, f32 = jnp.bfloat16, jnp.float32
    vmem = pl.BlockSpec(memory_space=pltpu.VMEM)
    hbm = pl.BlockSpec(memory_space=pltpu.HBM)
    dma = pltpu.SemaphoreType.DMA
    by_ctx, by_exp = dma((n_ctx,)), dma((n_exp,))
    both = dma((n_exp, n_ctx))
    return pl.pallas_call(
        functools.partial(kernel, n_ctx, n_exp),
        out_shape=(
            jax.ShapeDtypeStruct((block, heads * LATENT), bf16),
            jax.ShapeDtypeStruct((tokens, out_width), bf16),
        ),
        in_specs=[hbm] * 9,
        out_specs=(vmem, vmem),
        scratch_shapes=[
            pltpu.VMEM(queries.shape, bf16),
            pltpu.VMEM((LATENT + ROPE, block), bf16),
            pltpu.SMEM(block_order.shape, jnp.int32),
            pltpu.VMEM(moe_input.shape, bf16),
            pltpu.VMEM(routes.shape[::-1], jnp.int32),
            pltpu.VMEM(gate_weights.shape[::-1], f32),
            pltpu.VMEM(wg.shape, bf16),
            pltpu.VMEM(wu.shape, bf16),
            pltpu.VMEM(wd.shape, bf16),
            pltpu.VMEM((LATENT + ROPE, n_ctx * block), bf16),
            pltpu.VMEM((n_ctx * block, LATENT), bf16),
            pltpu.VMEM((n_ctx, 2, tokens // 2, width + LANES), bf16),
            pltpu.VMEM((n_exp, n_ctx, 2, tokens // 2, width + LANES), bf16),
            pltpu.VMEM((n_ctx, 2, (LATENT + ROPE) // 2, block), bf16),
            pltpu.VMEM((n_exp, slices, chunk, 2 * slice_width), bf16),
            pltpu.VMEM((n_exp, n_ctx, chunk, 2 * slice_width), bf16),
            pltpu.VMEM((n_exp, chunk, slice_width), bf16),
            pltpu.VMEM((n_exp, n_ctx, tokens, out_width), bf16),
            pltpu.VMEM((n_exp, n_ctx, tokens, out_width), bf16),
            pltpu.VMEM((n_exp, tokens, out_width), bf16),
            pltpu.VMEM((n_exp, tokens, out_width), bf16),
            pltpu.VMEM((tokens, out_width), f32),
            dma((9,)),
            by_ctx, by_ctx, by_exp, by_exp, by_exp, by_exp, by_ctx, by_ctx, dma, dma,
            dma((n_exp, slices)), both, by_exp, by_exp, both, both, by_exp, by_exp,
        ],
        compiler_params=pltpu.CompilerParams(
            collective_id=0, has_side_effects=True, vmem_limit_bytes=64 * 1024 * 1024
        ),
    )(
        queries, latent_keys.T, block_order, moe_input, routes.T, gate_weights.T, wg, wu, wd
    )


def passed_along(block, axis, distance):
    devices = range(lax.axis_size(axis))
    route = [((i - distance) % len(devices), i) for i in devices]
    return lax.ppermute(block, axis, route)


def slot_table(route_rows, experts, capacity):
    flat_ids = route_rows.reshape(-1)
    one_hot = (flat_ids[:, None] == jnp.arange(experts, dtype=jnp.int32)[None, :]).astype(jnp.int32)
    earlier = jnp.cumsum(one_hot, axis=0) - one_hot
    ranking = jnp.sum(earlier * one_hot, axis=1)
    return flat_ids * capacity + ranking


def body(queries, latent_keys, block_order, moe_input, routes, gate_weights, w_gate, w_up, w_down):
    full_gate, full_up, full_down = (
        lax.all_gather(w_gate, "ctx", axis=1, tiled=True),
        lax.all_gather(w_up, "ctx", axis=1, tiled=True),
        lax.all_gather(w_down, "ctx", axis=1, tiled=True),
    )
    full_width = LATENT + ROPE
    block_len = queries.shape[0]
    heads_here = queries.shape[1] // full_width
    per_head = queries.reshape(block_len, heads_here, full_width)
    cycle_size = lax.axis_size("ctx")
    position = lax.axis_index("ctx")
    offsets = jnp.arange(block_len, dtype=jnp.int32)
    own_block = block_order[position]
    own_pos = own_block * block_len + offsets

    def attend(running, key_block, source):
        source_block = block_order[source]
        top_old, total_old, summed_old = running
        key_pos = source_block * block_len + offsets
        visible = (key_pos[None, :] <= own_pos[:, None]) & True
        scores = (
            jnp.einsum("thc,uc->thu", per_head, key_block, preferred_element_type=jnp.float32)
            * softmax_scale
        )
        masked = jnp.where(visible[:, None, :], scores, very_negative)
        top_new = jnp.maximum(top_old, jnp.max(masked, axis=-1))
        weights = jnp.where(visible[:, None, :], jnp.exp(masked - top_new[:, :, None]), 0.0)
        factor = jnp.exp(top_old - top_new)
        total_new = total_old * factor + jnp.sum(weights, axis=-1)
        summed_new = summed_old * factor[:, :, None] + jnp.einsum(
            "thu,uc->thc",
            weights.astype(jnp.bfloat16),
            key_block[:, :LATENT],
            preferred_element_type=jnp.float32,
        )
        return (top_new, total_new, summed_new)

    initial = (
        jnp.full((block_len, heads_here), very_negative, jnp.float32),
        jnp.zeros((block_len, heads_here), jnp.float32),
        jnp.zeros((block_len, heads_here, LATENT), jnp.float32),
    )
    running = attend(initial, latent_keys, position)

    def step_forward(step_index, carried):
        state_now, ahead_keys = carried
        ahead_keys = passed_along(ahead_keys, "ctx", 1)
        state_now = attend(state_now, ahead_keys, (position - step_index) % cycle_size)
        return (state_now, ahead_keys)

    finished = lax.fori_loop(1, cycle_size, step_forward, (running, latent_keys))
    top_score, row_total, summed = finished[0]
    context = (
        (summed / row_total[:, :, None])
        .astype(jnp.bfloat16)
        .reshape(block_len, heads_here * LATENT)
    )
    tokens_here = moe_input.shape[0]
    top_count = routes.shape[1]
    owners = lax.axis_size("exp")
    experts = w_gate.shape[0] * owners
    capacity = min(tokens_here, 2 * tokens_here * top_count // experts)
    model_width = moe_input.shape[1]
    half_width = w_down.shape[2]
    slot_index = slot_table(routes, experts, capacity)
    outgoing = (
        jnp.zeros((experts * capacity, model_width), jnp.bfloat16)
        .at[slot_index]
        .set(jnp.repeat(moe_input, top_count, axis=0))
    )
    outgoing = outgoing.reshape(owners, capacity, model_width)
    arrived = lax.all_to_all(outgoing, "exp", split_axis=0, concat_axis=0, tiled=True)
    flat_rows = arrived.reshape(-1, model_width)
    gate_proj = jnp.dot(flat_rows, full_gate[0], preferred_element_type=jnp.float32)
    upward = jnp.dot(flat_rows, full_up[0], preferred_element_type=jnp.float32)
    hidden = (jax.nn.silu(gate_proj) * upward).astype(jnp.bfloat16)
    hidden_all = lax.all_gather(hidden, "tp", axis=1, tiled=True)
    produced_rows = jnp.dot(hidden_all, full_down[0], preferred_element_type=jnp.float32).astype(
        jnp.bfloat16
    )
    produced = produced_rows.reshape(arrived.shape[0], arrived.shape[1], half_width)
    returned = lax.all_to_all(produced, "exp", split_axis=0, concat_axis=0, tiled=True)
    picked = (
        returned.reshape(-1, half_width)[slot_index]
        .astype(jnp.float32)
        .reshape(tokens_here, top_count, half_width)
    )
    moe_out = jnp.sum(picked * gate_weights[:, :, None], axis=1).astype(jnp.bfloat16)
    return (context, moe_out)


def solution(mesh):
    in_specs = (
        P("ctx", ("exp", "tp")),
        P("ctx", None),
        P(),
        P(("ctx", "exp"), None),
        P(("ctx", "exp"), None),
        P(("ctx", "exp"), None),
        P("exp", "ctx", "tp"),
        P("exp", "ctx", "tp"),
        P("exp", "ctx", "tp"),
    )
    out_specs = (P("ctx", ("exp", "tp")), P(("ctx", "exp"), "tp"))
    n_ctx, n_exp, n_tp = mesh.shape["ctx"], mesh.shape["exp"], mesh.shape["tp"]

    def whole(*args):
        units_slice = args[8].shape[1] // n_ctx
        width = args[6].shape[1] // n_ctx
        fits = units_slice % LANES == 0 and width % LANES == 0 and n_ctx * n_exp <= 16 and n_exp > 2 and n_tp == 2
        inner = functools.partial(fused_body, n_ctx, n_exp) if fits else body
        return split(inner)(*args)

    def split(inner):
        return jax.shard_map(
            inner, mesh=mesh, in_specs=in_specs, out_specs=out_specs, check_vma=False
        )

    return whole
```
